32 devices in a mesh: grp: 2 (over x), area: 8 (over z, y), ctg: 2 (over core).
Axes of the slice: x: 2, y: 2, z: 4, core: 2. Of those that a mesh axis runs over, the one named last changes fastest.
Arguments:
- area_size: int32 [16], P(('grp', 'area')), parts along dimension 0, may hold values from 299 to 1024, as said below
- tie_peer: int32 [16, 42], P(('grp', 'area')), parts along dimension 0, may hold values from 0 to 7, as said below
- kkt_diag: float32 [16, 2, 1024], P(('grp', 'area'), 'ctg'), parts along dimension 0, may hold values from 0.5 to 1
- kkt_offdiag: float32 [16, 2, 1024, 1024], P(('grp', 'area'), 'ctg'), parts along dimension 0, may hold values from -0.1875 to 0.1875
- cost: float32 [16, 2, 1024, 256], P(('grp', 'area'), 'ctg'), parts along dimension 0, may hold values from -6 to 6
- consensus: float32 [16, 2, 1024, 256], P(('grp', 'area'), 'ctg'), parts along dimension 0, may hold values from -4 to 4
- dual: float32 [16, 2, 1024, 256], P(('grp', 'area'), 'ctg'), parts along dimension 0, may hold values from -4 to 4
- limit: float32 [16, 1024, 256], P(('grp', 'area')), parts along dimension 0, may hold values from 0.3 to 1.5
Outputs:
- agreed_out: float32 [16, 2, 1024, 256], P(('grp', 'area'), 'ctg'), parts along dimension 0
- dual_out: float32 [16, 2, 1024, 256], P(('grp', 'area'), 'ctg'), parts along dimension 0
The draws below stay inside these ranges and needn't reach their ends.
There are 2 independent parts, one for each index of `grp`. The reference program is written for one: setup_inputs(seed, part) draws one part's arguments, and reference() takes and returns one part's arrays. A program takes and returns all parts, laid end to end along the dimension named above; each array names one. Nothing has to cross between parts.
Inputs may be any that keep to these rules, and one draw needn't show every extreme that they name: `area_size`: some area has exactly 1024 live slots. `tie_peer`: never the area itself; each area has exactly 6 tie slots to each other area.
All inputs are finite; a program needn't handle non-finite values.
Results may differ from the reference program's by a relative error of at most 0.0003.
Values sent between devices are 32-bit elements; how exact they have to be, the bound alone decides.
A program may use at most 64 MiB of HBM per device.

```python
import math
import jax
import jax.numpy as jnp
from jax import lax

SLOTS = 1024
HOURS = 256
GENS = 256
TIE_PAIR = 6
ITERS = 3
N_AREA = 8
N_CTG = 2


def draw_area_size(key, part):
    first, second = jax.random.split(jax.random.fold_in(key, 11))
    lowest = GENS + TIE_PAIR * (N_AREA - 1) + 1
    sizes = jax.random.randint(first, (N_AREA,), lowest, SLOTS + 1)
    chosen = jax.random.randint(second, (), 0, N_AREA)
    return sizes.at[chosen].set(SLOTS).astype(jnp.int32)


def draw_tie_peer(key, part):
    ties = TIE_PAIR * (N_AREA - 1)
    subkeys = jax.random.split(jax.random.fold_in(key, 23), N_AREA)
    shuffled = jax.vmap(lambda single: jax.random.permutation(single, ties))(subkeys)
    areas = jnp.arange(N_AREA)[:, None]
    return ((areas + 1 + shuffled // TIE_PAIR) % N_AREA).astype(jnp.int32)


def level_of(key, shape, shards, least, high):
    def one(position, parts):
        heights = jax.random.uniform(jax.random.fold_in(jax.random.fold_in(key, 6), position), (parts,), jnp.float32, least / len(shards), high / len(shards))
        return jnp.repeat(jnp.exp(heights), shape[position] // parts).reshape((-1,) + (1,) * (len(shape) - position - 1))

    level = one(*shards[0])
    for cut in shards[1:]:
        level = level * one(*cut)
    return level


def centred(own_key, extent, deviation, most, shards=(), kind=jnp.bfloat16):
    values = deviation * jax.random.normal(own_key, extent, jnp.float32)
    if shards:
        values = values * level_of(own_key, extent, shards, -0.22, 0.18)
    return jnp.clip(values, -most, most).astype(kind)


def setup_inputs(seed: int = 0, part: int = 0) -> dict:
    arg_keys = jax.random.split(jax.random.key(seed), 9)
    part_keys = jax.random.split(jax.random.fold_in(arg_keys[8], part), 9)
    area_size = draw_area_size(jax.random.fold_in(jax.random.fold_in(arg_keys[8], part), 71), part)
    tie_peer = draw_tie_peer(jax.random.fold_in(jax.random.fold_in(arg_keys[8], part), 71), part)
    kkt_diag = jnp.clip(0.5 + 0.5 * jax.random.uniform(part_keys[2], (N_AREA, N_CTG, SLOTS), jnp.float32) ** level_of(part_keys[2], (N_AREA, N_CTG, SLOTS), ((0, 8), (1, 2)), -0.2, 0.2), 0.5, 1.0)
    kkt_offdiag = centred(part_keys[3], (N_AREA, N_CTG, SLOTS, SLOTS), SLOTS ** -0.5, 0.1875, ((0, 8), (1, 2)), jnp.float32)
    cost = centred(part_keys[4], (N_AREA, N_CTG, SLOTS, HOURS), 1.0, 6.0, ((0, 8), (1, 2)), jnp.float32)
    consensus = centred(part_keys[5], (N_AREA, N_CTG, SLOTS, HOURS), 0.5, 4.0, ((0, 8), (1, 2)), jnp.float32)
    dual = centred(part_keys[6], (N_AREA, N_CTG, SLOTS, HOURS), 0.5, 4.0, ((0, 8), (1, 2)), jnp.float32)
    limit = jnp.clip(jnp.exp(math.log(1.5) - 1.60943787 * jax.random.uniform(part_keys[7], (N_AREA, SLOTS, HOURS), jnp.float32) ** level_of(part_keys[7], (N_AREA, SLOTS, HOURS), ((0, 8),), -0.2, 0.2)), 0.3, 1.5)
    return dict(area_size=area_size, tie_peer=tie_peer, kkt_diag=kkt_diag, kkt_offdiag=kkt_offdiag, cost=cost, consensus=consensus, dual=dual, limit=limit)


def tie_dest(peers):
    count = peers.shape[0]
    order = jnp.arange(count)
    same = (peers[:, None] == peers[None, :]) & (order[:, None] < order[None, :])
    rank = jnp.sum(same.astype(jnp.int32), axis=0)
    return (peers * TIE_PAIR + rank).astype(jnp.int32)


def reference(area_size, tie_peer, kkt_diag, kkt_offdiag, cost, consensus, dual, limit):
    ties = TIE_PAIR * (N_AREA - 1)
    live = (jnp.arange(SLOTS)[None, :] < area_size[:, None]).astype(jnp.float32)[:, None, :, None]
    dest = jax.vmap(tie_dest)(tie_peer)
    bound = limit[:, None]
    agreed = consensus
    dual_var = dual

    def product(pieces):
        return jnp.einsum("cij,cjh->cih", pieces[0], pieces[1], precision=lax.Precision.HIGHEST)

    def scatter_one(values, where):
        return jnp.zeros((N_CTG, N_AREA * TIE_PAIR, HOURS), jnp.float32).at[:, where].set(values)

    def take_one(values, where):
        return values[:, where]

    for iteration in range(ITERS):
        right_side = live * (agreed - dual_var - cost)
        applied = lax.map(product, (kkt_offdiag, right_side))
        primal = live * (kkt_diag[..., None] * right_side + applied)
        shifted = primal + dual_var
        gen_mean = jnp.broadcast_to(jnp.mean(shifted[:, :, :GENS], axis=1, keepdims=True), (N_AREA, N_CTG, GENS, HOURS))
        tie_part = shifted[:, :, GENS:GENS + ties]
        sent = jax.vmap(scatter_one)(tie_part, dest)
        sent = sent.reshape(N_AREA, N_CTG, N_AREA, TIE_PAIR, HOURS)
        got = jnp.transpose(sent, (2, 1, 0, 3, 4)).reshape(N_AREA, N_CTG, N_AREA * TIE_PAIR, HOURS)
        other = jax.vmap(take_one)(got, dest)
        averaged = jnp.concatenate([gen_mean, 0.5 * (tie_part + other), shifted[:, :, GENS + ties:]], axis=2)
        agreed = live * jnp.clip(averaged, -bound, bound)
        dual_var = live * (dual_var + primal - agreed)
    return agreed, dual_var
```

```python
import functools

import jax
import jax.numpy as jnp
from jax import lax
from jax.experimental import pallas as pl
from jax.experimental.pallas import tpu as pltpu
from jax.sharding import PartitionSpec as P

GENS = 256
ITERS = 3
MESH = pl.DeviceIdType.MESH


def round_up(value, step):
    return (value + step - 1) // step * step


def fast_dot(a, b):
    return jnp.dot(a, b, preferred_element_type=jnp.float32)


def split_two(x):
    high = x.astype(jnp.bfloat16)
    low = (x - high.astype(jnp.float32)).astype(jnp.bfloat16)
    return high, low


def move_rows(one_hot, x):
    width = x.shape[1]
    high = x.astype(jnp.bfloat16)
    rest = x - high.astype(jnp.float32)
    mid = rest.astype(jnp.bfloat16)
    low = (rest - mid.astype(jnp.float32)).astype(jnp.bfloat16)
    out = fast_dot(one_hot, jnp.concatenate([high, mid, low], axis=1))
    return out[:, :width] + out[:, width:2 * width] + out[:, 2 * width:]


def kernel(
    areas, scenarios, ties, size_ref, peer_ref, diag_ref, k_hbm, cost_hbm, cons_hbm, dual_hbm,
    limit_hbm, agreed_hbm, dualout_hbm,
    k_ref, cost, cons, dual, limit, agreed, acc, k_top, k_bot, r_top, r_bot,
    pack, unpack, sent, got, gen_sent, gen_got,
    in_sems, out_sems, tie_send, tie_recv, gen_send, gen_recv,
):
    slots, hours = cost.shape
    pair_lines = ties // (areas - 1)
    pad_lines = sent.shape[2]
    split = k_top.shape[1] // 3
    head = GENS + round_up(ties, 16)
    tie_rows = head - GENS
    me = lax.axis_index("area")
    mine = lax.axis_index("ctg")

    barrier = pltpu.get_barrier_semaphore()
    step = round_up(-(-(slots - head) // 3), 16)
    chunks = [(0, head)] + [(a, min(a + step, slots)) for a in range(head, slots, step)]

    def load(src, dst, index):
        return pltpu.make_async_copy(src, dst, in_sems.at[index])

    loads = [
        load(cons_hbm.at[0, 0], cons, 0),
        load(dual_hbm.at[0, 0], dual, 1),
        load(cost_hbm.at[0, 0], cost, 2),
    ]
    k_loads = [
        load(k_hbm.at[0, 0, pl.ds(a, b - a)], k_ref.at[pl.ds(a, b - a)], 4 + j)
        for j, (a, b) in enumerate(chunks)
    ]
    limit_load = load(limit_hbm.at[0], limit, 3)
    for copy in loads:
        copy.start()
    for copy in k_loads:
        copy.start()
    limit_load.start()

    def each_peer(body):
        if areas <= 8:
            for o in range(areas - 1):
                body(o)
        else:
            lax.fori_loop(0, areas - 1, lambda o, c: (body(o), c)[1], 0)

    def greet(o):
        pl.semaphore_signal(
            barrier, inc=1, device_id={"area": lax.rem(me + o + 1, areas)}, device_id_type=MESH
        )

    each_peer(greet)
    for o in range(1, scenarios):
        pl.semaphore_signal(
            barrier, inc=1, device_id={"ctg": lax.rem(mine + o, scenarios)}, device_id_type=MESH
        )

    size = size_ref[0]

    def live_rows(a, b):
        return lax.broadcasted_iota(jnp.int32, (b - a, hours), 0) + a < size

    peers = jnp.concatenate(
        [peer_ref[...], jnp.full((1, tie_rows - ties), -1, jnp.int32)], axis=1
    ) if tie_rows > ties else peer_ref[...]
    row_id = lax.broadcasted_iota(jnp.int32, (tie_rows, tie_rows), 0)
    col_id = lax.broadcasted_iota(jnp.int32, (tie_rows, tie_rows), 1)
    across = jnp.broadcast_to(peers, (tie_rows, tie_rows))
    down = jnp.sum(jnp.where(row_id == col_id, across, 0), axis=1, keepdims=True)
    same = across == down
    rank_row = jnp.sum(jnp.where(same & (row_id < col_id), 1, 0), axis=0, keepdims=True)
    rank_col = jnp.sum(jnp.where(same & (col_id < row_id), 1, 0), axis=1, keepdims=True)

    def place(peer, rank):
        back = peer - me - 1
        turn = jnp.where(back < 0, back + areas, back)
        return jnp.where(peer < 0, -1, turn * pad_lines + rank)

    lanes = areas * pad_lines
    dest_row = place(peers, rank_row)
    dest_col = place(down, rank_col)
    pack[...] = jnp.where(
        lax.broadcasted_iota(jnp.int32, (lanes, tie_rows), 0) == dest_row, 1.0, 0.0
    ).astype(jnp.bfloat16)
    unpack[...] = jnp.where(
        lax.broadcasted_iota(jnp.int32, (tie_rows, lanes), 1) == dest_col, 1.0, 0.0
    ).astype(jnp.bfloat16)
    for it in range(ITERS):
        got[it, areas - 1] = jnp.zeros((pad_lines, hours), jnp.float32)

    def put_right(side, a, b, value):
        high, low = split_two(value)
        for lo, hi, ref in ((0, split, r_top), (split, slots, r_bot)):
            first, last = max(a, lo), min(b, hi)
            if first < last:
                span = hi - lo
                for j, part in enumerate((high, high, low)):
                    ref[side, j * span + first - lo:j * span + last - lo] = part[first - a:last - a]

    def convert(a, b):
        def body(g, carry):
            row = pl.multiple_of(a + g * 16, 16)
            first = pl.multiple_of(row // 128 * 128, 128)
            where = (pl.ds(row, 16), pl.ds(first, 128))
            on = lax.broadcasted_iota(jnp.int32, (16, 128), 0) + row == (
                lax.broadcasted_iota(jnp.int32, (16, 128), 1) + first
            )
            k_ref[where] = k_ref[where] + jnp.where(on, diag_ref[0, :, pl.ds(first, 128)], 0.0)
            high, low = split_two(k_ref[pl.ds(row, 16), :])
            for lo, hi, ref in ((0, split, k_top), (split, slots, k_bot)):
                span = hi - lo
                ref[pl.ds(row, 16), :span] = high[:, lo:hi]
                ref[pl.ds(row, 16), span:2 * span] = low[:, lo:hi]
                ref[pl.ds(row, 16), 2 * span:] = high[:, lo:hi]
            return carry

        lax.fori_loop(0, (b - a) // 16, body, 0)

    def product_of(it, a, b):
        near = fast_dot(k_top[a:b], r_top[it % 2])
        return near + (fast_dot(k_bot[a:b], r_bot[0]) if it == 0 else acc[a:b])

    def update(it, a, b, averaged, shifted):
        clipped = jnp.clip(averaged, -limit[a:b], limit[a:b])
        rest = shifted - clipped
        dual[a:b] = rest
        if it == ITERS - 1:
            agreed[a:b] = clipped
        else:
            put_right((it + 1) % 2, a, b, clipped - rest - cost[a:b])

    def tie_copy(it, o):
        return pltpu.make_async_remote_copy(
            src_ref=sent.at[it, o], dst_ref=got.at[it, areas - 2 - o],
            send_sem=tie_send.at[it], recv_sem=tie_recv.at[it],
            device_id={"area": lax.rem(me + o + 1, areas)}, device_id_type=MESH,
        )

    def tie_all(it):
        return pltpu.make_async_remote_copy(
            src_ref=sent.at[it, pl.ds(0, areas - 1)], dst_ref=got.at[it, pl.ds(0, areas - 1)],
            send_sem=tie_send.at[it], recv_sem=tie_recv.at[it],
            device_id={"area": lax.rem(me + 1, areas)}, device_id_type=MESH,
        )

    def gen_copy(it, o):
        return pltpu.make_async_remote_copy(
            src_ref=gen_sent.at[it], dst_ref=gen_got.at[it, o - 1],
            send_sem=gen_send.at[it, o - 1], recv_sem=gen_recv.at[it, o - 1],
            device_id={"ctg": lax.rem(mine + o, scenarios)}, device_id_type=MESH,
        )

    def send_ties(it, shifted):
        sent[it] = move_rows(pack[...], shifted).reshape(areas, pad_lines, hours)
        each_peer(lambda o: tie_copy(it, o).start())

    def out_copies(a, b, index):
        where = pl.ds(a, b - a)
        return [
            pltpu.make_async_copy(agreed.at[where], agreed_hbm.at[0, 0, where], out_sems.at[0, index]),
            pltpu.make_async_copy(dual.at[where], dualout_hbm.at[0, 0, where], out_sems.at[1, index]),
        ]

    for copy in loads:
        copy.wait()
    for a in range(0, slots, 128):
        b = min(a + 128, slots)
        live = live_rows(a, b)
        linear = jnp.where(live, cost[a:b], 0.0)
        cost[a:b] = linear
        put_right(0, a, b, jnp.where(live, cons[a:b] - dual[a:b], 0.0) - linear)

    for it in range(ITERS):
        last = it == ITERS - 1
        if it == 0:
            k_loads[0].wait()
            convert(0, head)
        for a, b in ((GENS, head), (0, GENS)):
            product = product_of(it, a, b)
            shifted = jnp.where(live_rows(a, b), product + dual[a:b], 0.0)
            if a == GENS:
                acc[a:b] = shifted
                if it == 0:
                    pl.semaphore_wait(barrier, areas - 1 + scenarios - 1)
                send_ties(it, shifted)
            else:
                gen_sent[it] = shifted
                for o in range(1, scenarios):
                    gen_copy(it, o).start()
        if it == 0:
            limit_load.wait()
        for j, (a, b) in enumerate(chunks[1:]):
            if it == 0:
                k_loads[j + 1].wait()
                convert(a, b)
            product = product_of(it, a, b)
            shifted = jnp.where(live_rows(a, b), product + dual[a:b], 0.0)
            update(it, a, b, shifted, shifted)
            if last:
                for copy in out_copies(a, b, j + 1):
                    copy.start()
        tie_shifted = acc[GENS:head]
        if not last:
            for a, b in chunks:
                acc[a:b] = fast_dot(k_bot[a:b], r_bot[(it + 1) % 2])
        for o in range(1, scenarios):
            gen_copy(it, o).wait_recv()
        own = gen_sent[it]
        total = own
        for o in range(1, scenarios):
            total = total + gen_got[it, o - 1]
        update(it, 0, GENS, total * (1.0 / scenarios), own)
        tie_all(it).wait_recv()
        other = move_rows(unpack[...], got[it].reshape(lanes, hours))
        is_tie = lax.broadcasted_iota(jnp.int32, (tie_rows, hours), 0) < ties
        averaged = jnp.where(is_tie, 0.5 * (tie_shifted + other), tie_shifted)
        update(it, GENS, head, averaged, tie_shifted)

    for copy in out_copies(0, head, 0):
        copy.start()
    for it in range(ITERS):
        tie_all(it).wait_send()
        for o in range(1, scenarios):
            gen_copy(it, o).wait_send()
    for j, (a, b) in enumerate(chunks):
        for copy in out_copies(a, b, j):
            copy.wait()


def local(area_size, tie_peer, kkt_diag, kkt_offdiag, cost, consensus, dual, limit):
    areas = lax.axis_size("area")
    scenarios = lax.axis_size("ctg")
    ties = tie_peer.shape[1]
    slots, hours = cost.shape[2:]
    pad_lines = round_up(ties // (areas - 1), 8)
    tie_rows = round_up(ties, 16)
    split = round_up(GENS + tie_rows, 256)
    f32, b16 = jnp.float32, jnp.bfloat16
    vmem = pltpu.VMEM
    whole = pl.BlockSpec(memory_space=vmem)
    far = pl.BlockSpec(memory_space=pltpu.HBM)
    dma = pltpu.SemaphoreType.DMA
    out = jax.ShapeDtypeStruct(cost.shape, f32)
    lanes = areas * pad_lines
    state = vmem((slots, hours), f32)
    return pl.pallas_call(
        functools.partial(kernel, areas, scenarios, ties),
        out_shape=(out, out),
        in_specs=[pl.BlockSpec(memory_space=pltpu.SMEM), whole, whole, far, far, far, far, far],
        out_specs=(far, far),
        scratch_shapes=[
            vmem((slots, slots), f32), state, state, state, state, state, state,
            vmem((slots, 3 * split), b16), vmem((slots, 3 * (slots - split)), b16),
            vmem((2, 3 * split, hours), b16), vmem((2, 3 * (slots - split), hours), b16),
            vmem((lanes, tie_rows), b16), vmem((tie_rows, lanes), b16),
            vmem((ITERS, areas, pad_lines, hours), f32),
            vmem((ITERS, areas, pad_lines, hours), f32),
            vmem((ITERS, GENS, hours), f32),
            vmem((ITERS, scenarios - 1, GENS, hours), f32),
            dma((8,)), dma((2, 4)), dma((ITERS,)), dma((ITERS,)),
            dma((ITERS, scenarios - 1)), dma((ITERS, scenarios - 1)),
        ],
        compiler_params=pltpu.CompilerParams(
            collective_id=0, has_side_effects=True, vmem_limit_bytes=48 * 1024 * 1024
        ),
    )(area_size, tie_peer, kkt_diag, kkt_offdiag, cost, consensus, dual, limit)


def solution(mesh):
    return jax.shard_map(
        local,
        mesh=mesh,
        in_specs=(
            P(("grp", "area")),
            P(("grp", "area"), None),
            P(("grp", "area"), "ctg", None),
            P(("grp", "area"), "ctg", None, None),
            P(("grp", "area"), "ctg", None, None),
            P(("grp", "area"), "ctg", None, None),
            P(("grp", "area"), "ctg", None, None),
            P(("grp", "area"), None, None),
        ),
        out_specs=(P(("grp", "area"), "ctg", None, None), P(("grp", "area"), "ctg", None, None)),
        check_vma=False,
    )
```

```python
import functools

import jax
import jax.numpy as jnp
from jax import lax
from jax.experimental import pallas as pl
from jax.experimental.pallas import tpu as pltpu
from jax.sharding import PartitionSpec as P

GENS = 256
ITERS = 3
MESH = pl.DeviceIdType.MESH


def round_up(value, step):
    return (value + step - 1) // step * step


def fast_dot(a, b):
    return jnp.dot(a, b, preferred_element_type=jnp.float32)


def split_two(x):
    high = x.astype(jnp.bfloat16)
    low = (x - high.astype(jnp.float32)).astype(jnp.bfloat16)
    return high, low


def move_rows(one_hot, x):
    width = x.shape[1]
    high = x.astype(jnp.bfloat16)
    rest = x - high.astype(jnp.float32)
    mid = rest.astype(jnp.bfloat16)
    low = (rest - mid.astype(jnp.float32)).astype(jnp.bfloat16)
    out = fast_dot(one_hot, jnp.concatenate([high, mid, low], axis=1))
    return out[:, :width] + out[:, width:2 * width] + out[:, 2 * width:]


def kernel(
    areas, scenarios, ties, size_hbm, peer_hbm, diag_hbm, k_hbm, cost_hbm, cons_hbm, dual_hbm,
    limit_hbm, agreed_out, dual_out,
    size_ref, peer_ref, diag_ref, k_ref, cost, cons, dual, limit, acc, k_top, k_bot, r_top, r_bot,
    pack, unpack, sent, got, gen_sent, gen_got,
    in_sems, tie_send, tie_recv, gen_send, gen_recv,
):
    slots, hours = cost.shape
    pair_lines = ties // (areas - 1)
    pad_lines = sent.shape[2]
    split = k_top.shape[1] // 3
    head = GENS + round_up(ties, 16)
    tie_rows = head - GENS
    me = lax.axis_index("area")
    mine = lax.axis_index("ctg")

    barrier = pltpu.get_barrier_semaphore()
    step = round_up(-(-(slots - head) // 3), 16)
    chunks = [(0, head)] + [(a, min(a + step, slots)) for a in range(head, slots, step)]

    def load(src, dst, index):
        return pltpu.make_async_copy(src, dst, in_sems.at[index])

    small_loads = [
        load(size_hbm, size_ref, 3),
        load(peer_hbm, peer_ref, 4),
        load(diag_hbm, diag_ref, 5),
    ]
    loads = [
        load(cons_hbm.at[0, 0], cons, 0),
        load(dual_hbm.at[0, 0], dual, 1),
        load(cost_hbm.at[0, 0], cost, 2),
    ]
    k_loads = [
        load(k_hbm.at[0, 0, pl.ds(a, b - a)], k_ref.at[pl.ds(a, b - a)], 7 + j)
        for j, (a, b) in enumerate(chunks)
    ]
    limit_load = load(limit_hbm.at[0], limit, 6)
    for copy in small_loads + loads:
        copy.start()
    for copy in k_loads:
        copy.start()
    limit_load.start()

    def each_peer(body):
        if areas <= 8:
            for o in range(areas - 1):
                body(o)
        else:
            lax.fori_loop(0, areas - 1, lambda o, c: (body(o), c)[1], 0)

    def greet(o):
        pl.semaphore_signal(
            barrier, inc=1, device_id={"area": lax.rem(me + o + 1, areas)}, device_id_type=MESH
        )

    each_peer(greet)
    for o in range(1, scenarios):
        pl.semaphore_signal(
            barrier, inc=1, device_id={"ctg": lax.rem(mine + o, scenarios)}, device_id_type=MESH
        )

    for copy in small_loads:
        copy.wait()
    size = size_ref[0]

    def live_rows(a, b):
        return lax.broadcasted_iota(jnp.int32, (b - a, hours), 0) + a < size

    peers = jnp.concatenate(
        [peer_ref[...], jnp.full((1, tie_rows - ties), -1, jnp.int32)], axis=1
    ) if tie_rows > ties else peer_ref[...]
    row_id = lax.broadcasted_iota(jnp.int32, (tie_rows, tie_rows), 0)
    col_id = lax.broadcasted_iota(jnp.int32, (tie_rows, tie_rows), 1)
    across = jnp.broadcast_to(peers, (tie_rows, tie_rows))
    down = jnp.sum(jnp.where(row_id == col_id, across, 0), axis=1, keepdims=True)
    same = across == down
    rank_row = jnp.sum(jnp.where(same & (row_id < col_id), 1, 0), axis=0, keepdims=True)
    rank_col = jnp.sum(jnp.where(same & (col_id < row_id), 1, 0), axis=1, keepdims=True)

    def place(peer, rank):
        back = peer - me - 1
        turn = jnp.where(back < 0, back + areas, back)
        return jnp.where(peer < 0, -1, turn * pad_lines + rank)

    lanes = areas * pad_lines
    dest_row = place(peers, rank_row)
    dest_col = place(down, rank_col)
    pack[...] = jnp.where(
        lax.broadcasted_iota(jnp.int32, (lanes, tie_rows), 0) == dest_row, 1.0, 0.0
    ).astype(jnp.bfloat16)
    unpack[...] = jnp.where(
        lax.broadcasted_iota(jnp.int32, (tie_rows, lanes), 1) == dest_col, 1.0, 0.0
    ).astype(jnp.bfloat16)
    for it in range(ITERS):
        got[it, areas - 1] = jnp.zeros((pad_lines, hours), jnp.float32)

    def put_right(side, a, b, value):
        high, low = split_two(value)
        for lo, hi, ref in ((0, split, r_top), (split, slots, r_bot)):
            first, last = max(a, lo), min(b, hi)
            if first < last:
                span = hi - lo
                for j, part in enumerate((high, high, low)):
                    ref[side, j * span + first - lo:j * span + last - lo] = part[first - a:last - a]

    def convert(a, b):
        groups = (b - a) // 16
        batch = max(m for m in (1, 2, 3, 4, 5) if groups % m == 0)

        def body(g, carry):
            for m in range(batch):
                rows_of(a + (g * batch + m) * 16)
            return carry

        def rows_of(row):
            row = pl.multiple_of(row, 16)
            first = pl.multiple_of(row // 128 * 128, 128)
            where = (pl.ds(row, 16), pl.ds(first, 128))
            on = lax.broadcasted_iota(jnp.int32, (16, 128), 0) + row == (
                lax.broadcasted_iota(jnp.int32, (16, 128), 1) + first
            )
            k_ref[where] = k_ref[where] + jnp.where(on, diag_ref[0, :, pl.ds(first, 128)], 0.0)
            high, low = split_two(k_ref[pl.ds(row, 16), :])
            for lo, hi, ref in ((0, split, k_top), (split, slots, k_bot)):
                span = hi - lo
                ref[pl.ds(row, 16), :span] = high[:, lo:hi]
                ref[pl.ds(row, 16), span:2 * span] = low[:, lo:hi]
                ref[pl.ds(row, 16), 2 * span:] = high[:, lo:hi]

        lax.fori_loop(0, groups // batch, body, 0)

    def product_of(it, a, b):
        near = fast_dot(k_top[a:b], r_top[it % 2])
        return near + (fast_dot(k_bot[a:b], r_bot[0]) if it == 0 else acc[a:b])

    def update(it, a, b, averaged, shifted):
        clipped = jnp.clip(averaged, -limit[a:b], limit[a:b])
        rest = shifted - clipped
        if it == ITERS - 1:
            agreed_out[0, 0, a:b] = clipped
            dual_out[0, 0, a:b] = rest
        else:
            dual[a:b] = rest
            put_right((it + 1) % 2, a, b, clipped - rest - cost[a:b])

    def tie_copy(it, o):
        return pltpu.make_async_remote_copy(
            src_ref=sent.at[it, o], dst_ref=got.at[it, areas - 2 - o],
            send_sem=tie_send.at[it], recv_sem=tie_recv.at[it],
            device_id={"area": lax.rem(me + o + 1, areas)}, device_id_type=MESH,
        )

    def tie_all(it):
        return pltpu.make_async_remote_copy(
            src_ref=sent.at[it, pl.ds(0, areas - 1)], dst_ref=got.at[it, pl.ds(0, areas - 1)],
            send_sem=tie_send.at[it], recv_sem=tie_recv.at[it],
            device_id={"area": lax.rem(me + 1, areas)}, device_id_type=MESH,
        )

    def gen_copy(it, o):
        return pltpu.make_async_remote_copy(
            src_ref=gen_sent.at[it], dst_ref=gen_got.at[it, o - 1],
            send_sem=gen_send.at[it, o - 1], recv_sem=gen_recv.at[it, o - 1],
            device_id={"ctg": lax.rem(mine + o, scenarios)}, device_id_type=MESH,
        )

    def send_ties(it, shifted):
        sent[it] = move_rows(pack[...], shifted).reshape(areas, pad_lines, hours)
        each_peer(lambda o: tie_copy(it, o).start())

    for copy in loads:
        copy.wait()
    for a in range(0, slots, 128):
        b = min(a + 128, slots)
        live = live_rows(a, b)
        linear = jnp.where(live, cost[a:b], 0.0)
        cost[a:b] = linear
        put_right(0, a, b, jnp.where(live, cons[a:b] - dual[a:b], 0.0) - linear)

    for it in range(ITERS):
        last = it == ITERS - 1
        if it == 0:
            k_loads[0].wait()
            convert(GENS, head)
            convert(0, GENS)
        for a, b in ((GENS, head), (0, GENS)):
            product = product_of(it, a, b)
            shifted = jnp.where(live_rows(a, b), product + dual[a:b], 0.0)
            if a == GENS:
                acc[a:b] = shifted
                if it == 0:
                    pl.semaphore_wait(barrier, areas - 1 + scenarios - 1)
                send_ties(it, shifted)
            else:
                gen_sent[it] = shifted
                for o in range(1, scenarios):
                    gen_copy(it, o).start()
        if it == 0:
            limit_load.wait()
        for j, (a, b) in enumerate(chunks[1:]):
            if it == 0:
                k_loads[j + 1].wait()
                convert(a, b)
            product = product_of(it, a, b)
            shifted = jnp.where(live_rows(a, b), product + dual[a:b], 0.0)
            update(it, a, b, shifted, shifted)
        tie_shifted = acc[GENS:head]
        if not last:
            for a, b in chunks:
                acc[a:b] = fast_dot(k_bot[a:b], r_bot[(it + 1) % 2])
        for o in range(1, scenarios):
            gen_copy(it, o).wait_recv()
        own = gen_sent[it]
        total = own
        for o in range(1, scenarios):
            total = total + gen_got[it, o - 1]
        update(it, 0, GENS, total * (1.0 / scenarios), own)
        tie_all(it).wait_recv()
        other = move_rows(unpack[...], got[it].reshape(lanes, hours))
        is_tie = lax.broadcasted_iota(jnp.int32, (tie_rows, hours), 0) < ties
        averaged = jnp.where(is_tie, 0.5 * (tie_shifted + other), tie_shifted)
        update(it, GENS, head, averaged, tie_shifted)

    for it in range(ITERS):
        tie_all(it).wait_send()
        for o in range(1, scenarios):
            gen_copy(it, o).wait_send()

def flush(agreed, dual, agreed_hbm, dual_hbm, sems):
    slots = agreed.shape[2]
    pieces = 4
    step = slots // pieces
    copies = []
    for j in range(pieces):
        where = (0, 0, pl.ds(j * step, step))
        copies.append(pltpu.make_async_copy(agreed.at[where], agreed_hbm.at[where], sems.at[0, j]))
        copies.append(pltpu.make_async_copy(dual.at[where], dual_hbm.at[where], sems.at[1, j]))
    for copy in copies:
        copy.start()
    for copy in copies:
        copy.wait()


def local(area_size, tie_peer, kkt_diag, kkt_offdiag, cost, consensus, dual, limit):
    areas = lax.axis_size("area")
    scenarios = lax.axis_size("ctg")
    ties = tie_peer.shape[1]
    slots, hours = cost.shape[2:]
    pad_lines = round_up(ties // (areas - 1), 8)
    tie_rows = round_up(ties, 16)
    split = round_up(GENS + tie_rows, 256)
    f32, b16 = jnp.float32, jnp.bfloat16
    vmem = pltpu.VMEM
    far = pl.BlockSpec(memory_space=pltpu.HBM)
    dma = pltpu.SemaphoreType.DMA
    out = jax.ShapeDtypeStruct(cost.shape, f32)
    near = pltpu.VMEM(cost.shape, f32)
    lanes = areas * pad_lines
    state = vmem((slots, hours), f32)
    agreed, dual_var = pl.pallas_call(
        functools.partial(kernel, areas, scenarios, ties),
        out_shape=(near, near),
        in_specs=[far] * 8,
        out_specs=(pl.BlockSpec(memory_space=vmem),) * 2,
        scratch_shapes=[
            pltpu.SMEM((1,), jnp.int32), vmem(tie_peer.shape, jnp.int32), vmem(kkt_diag.shape, f32),
            vmem((slots, slots), f32), state, state, state, state, state,
            vmem((slots, 3 * split), b16), vmem((slots, 3 * (slots - split)), b16),
            vmem((2, 3 * split, hours), b16), vmem((2, 3 * (slots - split), hours), b16),
            vmem((lanes, tie_rows), b16), vmem((tie_rows, lanes), b16),
            vmem((ITERS, areas, pad_lines, hours), f32),
            vmem((ITERS, areas, pad_lines, hours), f32),
            vmem((ITERS, GENS, hours), f32),
            vmem((ITERS, scenarios - 1, GENS, hours), f32),
            dma((11,)), dma((ITERS,)), dma((ITERS,)),
            dma((ITERS, scenarios - 1)), dma((ITERS, scenarios - 1)),
        ],
        compiler_params=pltpu.CompilerParams(
            collective_id=0, has_side_effects=True, vmem_limit_bytes=60 * 1024 * 1024
        ),
    )(area_size, tie_peer, kkt_diag, kkt_offdiag, cost, consensus, dual, limit)
    anywhere = pl.BlockSpec(memory_space=vmem)
    return pl.pallas_call(
        flush,
        out_shape=(out, out),
        in_specs=[anywhere] * 2,
        out_specs=(far, far),
        scratch_shapes=[dma((2, 4))],
    )(*[pltpu.with_memory_space_constraint(x, pltpu.VMEM) for x in (agreed, dual_var)])


def solution(mesh):
    return jax.shard_map(
        local,
        mesh=mesh,
        in_specs=(
            P(("grp", "area")),
            P(("grp", "area"), None),
            P(("grp", "area"), "ctg", None),
            P(("grp", "area"), "ctg", None, None),
            P(("grp", "area"), "ctg", None, None),
            P(("grp", "area"), "ctg", None, None),
            P(("grp", "area"), "ctg", None, None),
            P(("grp", "area"), None, None),
        ),
        out_specs=(P(("grp", "area"), "ctg", None, None), P(("grp", "area"), "ctg", None, None)),
        check_vma=False,
    )
```
